32 devices in a mesh: row: 8 (over z, y), feat: 4 (over x, core).
Axes of the slice: x: 2, y: 2, z: 4, core: 2. Of those that a mesh axis runs over, the one named last changes fastest.
Arguments:
- features: bfloat16 [28672, 512], P('row', 'feat'), may hold values from -6 to 6
- blocks: bfloat16 [896, 128, 128], P('row', 'feat'), may hold values from -0.3125 to 0.3125
- block_ptr: int32 [8, 29], P('row'), may hold values from 0 to 112, as said below
- block_col: int32 [8, 112], P('row'), may hold values from -1 to 223, as said below
- held_out: int32 [8, 128], P('row'), may hold values from 0 to 3583, as said below
- weight: bfloat16 [512, 512], P(None, 'feat'), may hold values from -0.25 to 0.25
- cotangent: bfloat16 [28672, 512], P('row', 'feat'), may hold values from -6 to 6
Outputs:
- layer_out: bfloat16 [28672, 512], P('row', 'feat')
- feature_grad: bfloat16 [28672, 512], P('row', 'feat')
- weight_grad: float32 [512, 512], P(None, 'feat')
The draws below stay inside these ranges and needn't reach their ends.
Inputs may be any that keep to these rules, and one draw needn't show every extreme that they name: `block_ptr`: each row is nondecreasing from 0; entry 28 is the shard's number of live slots, at least 98, and 112 in some shard. `block_col`: live slots of one shard name distinct blocks, at most 14 of them in any one shard; slots at or past the live count hold -1. `held_out`: the 128 numbers of a row are distinct.
All inputs are finite; a program needn't handle non-finite values.
Results may differ from the reference program's by a relative error of at most 0.0057.
Values may be sent and summed in bfloat16 or wider, within the bound.
A program may use at most 64 MiB of HBM per device.

```python
import jax
import jax.numpy as jnp
from jax import lax

BS = 128
F = 512
RB = 28
NB = 112
HELD = 128
SHARDS = 8
PEER_CAP = 14
CELLS = 28672


def layout(key):
    keys = jax.random.split(jax.random.fold_in(key, 11), 5)
    lowest = 7 * NB // 8
    counts = jax.random.randint(keys[0], (SHARDS,), lowest, NB + 1)
    full_at = jax.random.randint(keys[1], (), 0, SHARDS)
    counts = jnp.where(jnp.arange(SHARDS) == full_at, NB, counts)
    slots = jnp.arange(NB)
    live = slots[None, :] < counts[:, None]
    rows = jnp.sort(jax.random.randint(keys[2], (SHARDS, NB), 0, RB), axis=1)
    rows = jnp.where(live, rows, RB)
    pointers = jnp.sum((rows[:, :, None] < jnp.arange(RB + 1)[None, None, :]).astype(jnp.int32), axis=1)
    tickets = SHARDS * PEER_CAP
    scores = jax.random.randint(keys[3], (SHARDS, tickets), 0, 2 ** 20) * tickets + jnp.arange(tickets)[None, :]
    order = jnp.argsort(scores, axis=1)[:, :NB]
    source = order // PEER_CAP
    within = order % PEER_CAP
    offsets = jax.random.randint(keys[4], (SHARDS, SHARDS), 0, RB)
    offset = jnp.take_along_axis(offsets, source, axis=1)
    local = (offset + within) % RB
    columns = jnp.where(live, source * RB + local, -1)
    return (pointers.astype(jnp.int32), columns.astype(jnp.int32))


def draw_block_ptr(key, part):
    return layout(key)[0]


def draw_block_col(key, part):
    return layout(key)[1]


def draw_held_out(key, part):
    span = RB * BS
    scores = jax.random.randint(jax.random.fold_in(key, 23), (SHARDS, span), 0, 2 ** 20) * span + jnp.arange(span)[None, :]
    return jnp.argsort(scores, axis=1)[:, :HELD].astype(jnp.int32)


def level_of(stream_key, extent, cuts, low, top_value):
    level = 1.0
    for axis_at, shards_of in cuts:
        steps = jax.random.uniform(jax.random.fold_in(jax.random.fold_in(stream_key, 6), axis_at), (shards_of,), jnp.float32, low / len(cuts), top_value / len(cuts))
        level = level * jnp.repeat(jnp.exp(steps), extent[axis_at] // shards_of).reshape((-1,) + (1,) * (len(extent) - 1 - axis_at))
    return level


def gaussian(stream_key, extent, spread, limit, pieces=(), kind=jnp.bfloat16):
    drawn = jax.random.normal(stream_key, extent, jnp.float32) * spread
    if len(pieces) > 0:
        drawn = level_of(stream_key, extent, pieces, -0.22, 0.18) * drawn
    return jnp.clip(drawn, min=-limit, max=limit).astype(kind)


def setup_inputs(seed: int = 0) -> dict:
    seeds = jax.random.split(jax.random.key(seed), 8)
    return {
        "features": gaussian(seeds[0], (CELLS, F), 1.0, 6.0, ((0, 8), (1, 4))),
        "blocks": gaussian(seeds[1], (SHARDS * NB, BS, BS), (3 * BS) ** -0.5, 0.3125, ((0, 8), (1, 4))),
        "block_ptr": draw_block_ptr(jax.random.fold_in(seeds[7], 71), 0),
        "block_col": draw_block_col(jax.random.fold_in(seeds[7], 71), 0),
        "held_out": draw_held_out(jax.random.fold_in(seeds[7], 71), 0),
        "weight": gaussian(seeds[5], (F, F), F ** -0.5, 0.25, ((1, 4),)),
        "cotangent": gaussian(seeds[6], (CELLS, F), 1.0, 6.0, ((0, 8), (1, 4))),
    }


def slot_meta(ptr, col):
    slots = jnp.arange(NB, dtype=jnp.int32)
    live = slots < ptr[RB]
    brow = lax.optimization_barrier(jnp.sum((slots[:, None] >= ptr[None, 1:RB]).astype(jnp.int32), axis=1)).astype(jnp.int32)
    colc = jnp.where(live, col, 0).astype(jnp.int32)
    return (live, brow, colc)

def reference(features, blocks, block_ptr, block_col, held_out, weight, cotangent):
    shard_rows = RB * BS
    cell_ids = jnp.arange(shard_rows, dtype=jnp.int32)
    hits = jnp.any(cell_ids[None, :, None] == held_out[:, None, :], axis=2)
    keep = jnp.logical_not(hits.reshape(CELLS))
    kept = jnp.where(keep[:, None], features, jnp.zeros_like(features))
    kept_blocks = kept.reshape(SHARDS * RB, BS, F)
    block_sets = blocks.reshape(SHARDS, NB, BS, BS)

    def forward_shard(packed):
        mats, ptr, col = packed
        live, brow, colc = slot_meta(ptr, col)
        fetched = kept_blocks[colc].astype(jnp.float32)
        prods = jnp.einsum('kij,kjf->kif', mats.astype(jnp.float32), fetched)
        select = ((brow[None, :] == jnp.arange(RB, dtype=jnp.int32)[:, None]) & live[None, :]).astype(jnp.float32)
        summed = jnp.einsum('bk,kif->bif', select, prods, precision=lax.Precision.HIGHEST)
        return summed.reshape(shard_rows, F).astype(features.dtype)
    aggregated = lax.map(forward_shard, (block_sets, block_ptr, block_col)).reshape(CELLS, F)
    layer_out = jnp.dot(aggregated, weight, preferred_element_type=jnp.float32).astype(features.dtype)
    raw_grad = lax.dot_general(aggregated, cotangent, (((0,), (0,)), ((), ())), preferred_element_type=jnp.float32)
    weight_grad = raw_grad * (1.0 / jnp.sqrt(jnp.float32(CELLS)))
    agg_grad = jnp.dot(cotangent, weight.T, preferred_element_type=jnp.float32).astype(features.dtype)
    grad_blocks = agg_grad.reshape(SHARDS, RB, BS, F)

    def adjoint_step(total, packed):
        mats, ptr, col, grads = packed
        live, brow, colc = slot_meta(ptr, col)
        rows_in = grads[brow].astype(jnp.float32)
        contrib = jnp.einsum('kji,kjf->kif', mats.astype(jnp.float32), rows_in).astype(features.dtype)
        contrib = lax.optimization_barrier(contrib).astype(jnp.float32)
        contrib = jnp.where(live[:, None, None], contrib, jnp.zeros_like(contrib))
        return (total.at[colc].add(contrib), None)
    start = jnp.zeros((SHARDS * RB, BS, F), jnp.float32)
    summed, unused = lax.scan(adjoint_step, start, (block_sets, block_ptr, block_col, grad_blocks))
    summed = summed.reshape(CELLS, F)
    feature_grad = jnp.where(keep[:, None], summed, jnp.zeros_like(summed)).astype(features.dtype)
    return (layer_out, feature_grad, weight_grad)
```

```python
import jax
import jax.numpy as jnp
from jax import lax
from jax.experimental import pallas as pl
from jax.experimental.pallas import tpu as pltpu
from jax.sharding import PartitionSpec as P

VMEM_LIMIT = 40 * 2**20


def local_call(kernel, scalars, operands, out_shape, scratch=(), flops=0):
    moved = sum(o.size * o.dtype.itemsize for o in operands)
    moved += out_shape.size * out_shape.dtype.itemsize
    return pl.pallas_call(
        kernel,
        out_shape=out_shape,
        grid_spec=pltpu.PrefetchScalarGridSpec(
            num_scalar_prefetch=len(scalars),
            grid=(),
            in_specs=[pl.BlockSpec(memory_space=pltpu.VMEM)] * len(operands),
            out_specs=pl.BlockSpec(memory_space=pltpu.VMEM),
            scratch_shapes=list(scratch),
        ),
        compiler_params=pltpu.CompilerParams(vmem_limit_bytes=VMEM_LIMIT),
        cost_estimate=pl.CostEstimate(flops=flops, bytes_accessed=moved, transcendentals=0),
    )(*scalars, *operands)


def held_rows(held_ref, b, block_size):
    held = held_ref[...]
    ids = b * block_size + lax.broadcasted_iota(jnp.int32, (block_size, held.shape[1]), 0)
    return jnp.max((ids == held).astype(jnp.float32), axis=1, keepdims=True) > 0.5


def pack_kernel(asked_ref, held_ref, features_ref, out_ref, kept_ref):
    block_rows, block_size, _ = features_ref.shape

    def keep(b, carry):
        rows = features_ref[b].astype(jnp.float32)
        hit = held_rows(held_ref, b, block_size)
        kept_ref[b] = jnp.where(hit, 0.0, rows).astype(kept_ref.dtype)
        return carry

    lax.fori_loop(0, block_rows, keep, 0, unroll=4)

    def copy(p, carry):
        out_ref[p] = kept_ref[jnp.maximum(asked_ref[p], 0)]
        return carry

    lax.fori_loop(0, out_ref.shape[0], copy, 0, unroll=8)


def forward_kernel(position_ref, brow_ref, blocks_ref, arrived_ref, out_ref, acc_ref):
    slot_count = blocks_ref.shape[0]
    acc_ref[...] = jnp.zeros_like(acc_ref)

    def step(g, carry):
        slots = [g * UNROLL + i for i in range(UNROLL)]
        parts = [
            jnp.dot(blocks_ref[k], arrived_ref[position_ref[k]], preferred_element_type=jnp.float32)
            for k in slots
        ]
        for k, part in zip(slots, parts):
            acc_ref[brow_ref[k]] += part
        return carry

    lax.fori_loop(0, slot_count // UNROLL, step, 0)
    for k in range(slot_count // UNROLL * UNROLL, slot_count):
        acc_ref[brow_ref[k]] += jnp.dot(
            blocks_ref[k], arrived_ref[position_ref[k]], preferred_element_type=jnp.float32
        )

    def emit(b, carry):
        out_ref[b] = acc_ref[b].astype(out_ref.dtype)
        return carry

    lax.fori_loop(0, out_ref.shape[0], emit, 0, unroll=4)


UNROLL = 8


def contribution_kernel(slot_ref, brow_ref, blocks_ref, grad_ref, out_ref):
    def one(p):
        out_ref[p] = lax.dot_general(
            blocks_ref[slot_ref[p]],
            grad_ref[brow_ref[p]],
            (((0,), (0,)), ((), ())),
            preferred_element_type=jnp.float32,
        ).astype(out_ref.dtype)

    def step(p, carry):
        one(p)
        return carry

    lax.fori_loop(0, out_ref.shape[0], step, 0, unroll=8)


def collect_kernel(asked_ref, held_ref, returned_ref, out_ref, acc_ref):
    block_rows, block_size, _ = out_ref.shape
    acc_ref[...] = jnp.zeros_like(acc_ref)

    def add(p, carry):
        to = jnp.where(asked_ref[p] < 0, block_rows, asked_ref[p])
        acc_ref[to] += returned_ref[p].astype(jnp.float32)
        return carry

    lax.fori_loop(0, returned_ref.shape[0], add, 0, unroll=8)

    def emit(b, carry):
        hit = held_rows(held_ref, b, block_size)
        out_ref[b] = jnp.where(hit, 0.0, acc_ref[b]).astype(out_ref.dtype)
        return carry

    lax.fori_loop(0, block_rows, emit, 0, unroll=4)


def body(features, blocks, block_ptr, block_col, held_out, weight, cotangent):
    shards = lax.axis_size("row")
    my_feat = lax.axis_index("feat")
    rows_dev, width_dev = features.shape
    slot_count = blocks.shape[0]
    block_size = blocks.shape[2]
    block_rows = block_ptr.shape[1] - 1
    peer_cap = (slot_count + shards - 1) // shards
    buffer_len = shards * peer_cap
    bf16, f32 = jnp.bfloat16, jnp.float32

    slots = jnp.arange(slot_count, dtype=jnp.int32)
    live = slots < block_ptr[0, block_rows]
    columns = block_col[0]
    source = jnp.where(live, columns // block_rows, 0)
    local = jnp.where(live, columns % block_rows, 0)
    block_row = jnp.sum(
        (slots[:, None] >= block_ptr[0, 1:block_rows][None, :]).astype(jnp.int32), axis=1
    )
    earlier = (
        (source[:, None] == source[None, :]) & live[None, :] & (slots[None, :] < slots[:, None])
    )
    rank = jnp.sum(earlier.astype(jnp.int32), axis=1)
    position = jnp.where(live, source * peer_cap + rank, -1)
    places = jnp.arange(buffer_len, dtype=jnp.int32)
    match = (places[:, None] == position[None, :]).astype(jnp.int32)
    wanted = jnp.sum(match * (local[None, :] + 1), axis=1) - 1
    slot_at = jnp.sum(match * slots[None, :], axis=1)
    brow_at = jnp.sum(match * block_row[None, :], axis=1)
    asked = lax.all_to_all(wanted, "row", split_axis=0, concat_axis=0, tiled=True)

    full_blocks = lax.all_gather(blocks, "feat", axis=1, tiled=True)
    block_shape = (block_size, width_dev)
    outgoing = local_call(
        pack_kernel,
        (asked,),
        (held_out, features.reshape(block_rows, *block_shape)),
        jax.ShapeDtypeStruct((buffer_len, *block_shape), bf16),
        (pltpu.VMEM((block_rows, *block_shape), bf16),),
    )
    arrived = lax.all_to_all(outgoing, "row", split_axis=0, concat_axis=0, tiled=True)

    cot_piece = lax.all_gather(cotangent, "feat", axis=1, tiled=True)
    weight_piece = lax.all_gather(weight, "feat", axis=1, tiled=True)
    weight_mine = lax.dynamic_slice_in_dim(weight_piece, my_feat * width_dev, width_dev, 0)
    agg_grad = lax.dot_general(
        cot_piece, weight_mine, (((1,), (1,)), ((), ())), preferred_element_type=f32
    ).astype(bf16)
    sending = local_call(
        contribution_kernel,
        (slot_at, brow_at),
        (full_blocks, agg_grad.reshape(block_rows, *block_shape)),
        jax.ShapeDtypeStruct((buffer_len, *block_shape), bf16),
        flops=2 * buffer_len * block_size * block_size * width_dev,
    )
    returned = lax.all_to_all(sending, "row", split_axis=0, concat_axis=0, tiled=True)

    aggregated = local_call(
        forward_kernel,
        (jnp.maximum(position, 0), jnp.where(live, block_row, block_rows)),
        (full_blocks, arrived),
        jax.ShapeDtypeStruct((block_rows, *block_shape), bf16),
        (pltpu.VMEM((block_rows + 1, *block_shape), f32),),
        flops=2 * slot_count * block_size * block_size * width_dev,
    ).reshape(rows_dev, width_dev)
    piece = lax.all_gather(aggregated, "feat", axis=1, tiled=True)
    layer_out = jnp.dot(piece, weight, preferred_element_type=f32).astype(bf16)
    grad_part = lax.dot_general(
        piece, cotangent, (((0,), (0,)), ((), ())), preferred_element_type=f32
    )
    grad_total = lax.psum(grad_part, "row")
    weight_grad = grad_total * (1.0 / jnp.sqrt(f32(rows_dev * shards)))

    feature_grad = local_call(
        collect_kernel,
        (asked,),
        (held_out, returned),
        jax.ShapeDtypeStruct((block_rows, *block_shape), bf16),
        (pltpu.VMEM((block_rows + 1, *block_shape), f32),),
    ).reshape(rows_dev, width_dev)
    return (layer_out, feature_grad, weight_grad)


def solution(mesh):
    in_specs = (
        P("row", "feat"),
        P("row", "feat", None),
        P("row", None),
        P("row", None),
        P("row", None),
        P(None, "feat"),
        P("row", "feat"),
    )
    out_specs = (P("row", "feat"), P("row", "feat"), P(None, "feat"))
    return jax.shard_map(body, mesh=mesh, in_specs=in_specs, out_specs=out_specs, check_vma=False)
```

```python
import jax
import jax.numpy as jnp
from jax import lax
from jax.experimental import pallas as pl
from jax.experimental.pallas import tpu as pltpu
from jax.sharding import PartitionSpec as P

VMEM_LIMIT = 40 * 2**20


def local_call(kernel, scalars, operands, out_shape, scratch=(), flops=0):
    moved = sum(o.size * o.dtype.itemsize for o in operands)
    moved += out_shape.size * out_shape.dtype.itemsize
    return pl.pallas_call(
        kernel,
        out_shape=out_shape,
        grid_spec=pltpu.PrefetchScalarGridSpec(
            num_scalar_prefetch=len(scalars),
            grid=(),
            in_specs=[pl.BlockSpec(memory_space=pltpu.VMEM)] * len(operands),
            out_specs=pl.BlockSpec(memory_space=pltpu.VMEM),
            scratch_shapes=list(scratch),
        ),
        compiler_params=pltpu.CompilerParams(vmem_limit_bytes=VMEM_LIMIT),
        cost_estimate=pl.CostEstimate(flops=flops, bytes_accessed=moved, transcendentals=0),
    )(*scalars, *operands)


def held_rows(held_ref, b, block_size):
    held = held_ref[...]
    ids = b * block_size + lax.broadcasted_iota(jnp.int32, (block_size, held.shape[1]), 0)
    return jnp.max((ids == held).astype(jnp.float32), axis=1, keepdims=True) > 0.5


def pack_kernel(asked_ref, held_ref, features_ref, out_ref, kept_ref):
    block_rows, block_size, _ = features_ref.shape

    def keep(b, carry):
        rows = features_ref[b].astype(jnp.float32)
        hit = held_rows(held_ref, b, block_size)
        kept_ref[b] = jnp.where(hit, 0.0, rows).astype(kept_ref.dtype)
        return carry

    lax.fori_loop(0, block_rows, keep, 0, unroll=4)

    def copy(p, carry):
        out_ref[p] = kept_ref[jnp.maximum(asked_ref[p], 0)]
        return carry

    lax.fori_loop(0, out_ref.shape[0], copy, 0, unroll=8)


def forward_kernel(position_ref, brow_ref, blocks_ref, arrived_ref, out_ref, acc_ref):
    slot_count = blocks_ref.shape[0]
    acc_ref[...] = jnp.zeros_like(acc_ref)

    def step(g, carry):
        slots = [g * UNROLL + i for i in range(UNROLL)]
        parts = [
            jnp.dot(blocks_ref[k], arrived_ref[position_ref[k]], preferred_element_type=jnp.float32)
            for k in slots
        ]
        for k, part in zip(slots, parts):
            acc_ref[brow_ref[k]] += part
        return carry

    lax.fori_loop(0, slot_count // UNROLL, step, 0)
    for k in range(slot_count // UNROLL * UNROLL, slot_count):
        acc_ref[brow_ref[k]] += jnp.dot(
            blocks_ref[k], arrived_ref[position_ref[k]], preferred_element_type=jnp.float32
        )

    def emit(b, carry):
        out_ref[b] = acc_ref[b].astype(out_ref.dtype)
        return carry

    lax.fori_loop(0, out_ref.shape[0], emit, 0, unroll=4)


UNROLL = 8


def contribution_kernel(slot_ref, brow_ref, blocks_ref, grad_ref, out_ref):
    def one(p):
        out_ref[p] = lax.dot_general(
            blocks_ref[slot_ref[p]],
            grad_ref[brow_ref[p]],
            (((0,), (0,)), ((), ())),
            preferred_element_type=jnp.float32,
        ).astype(out_ref.dtype)

    def step(p, carry):
        one(p)
        return carry

    lax.fori_loop(0, out_ref.shape[0], step, 0, unroll=8)


def collect_kernel(asked_ref, held_ref, returned_ref, out_ref, acc_ref):
    block_rows, block_size, _ = out_ref.shape
    acc_ref[...] = jnp.zeros_like(acc_ref)

    def add(p, carry):
        to = jnp.where(asked_ref[p] < 0, block_rows, asked_ref[p])
        acc_ref[to] += returned_ref[p].astype(jnp.float32)
        return carry

    lax.fori_loop(0, returned_ref.shape[0], add, 0, unroll=8)

    def emit(b, carry):
        hit = held_rows(held_ref, b, block_size)
        out_ref[b] = jnp.where(hit, 0.0, acc_ref[b]).astype(out_ref.dtype)
        return carry

    lax.fori_loop(0, block_rows, emit, 0, unroll=4)


def sum_kernel(shards, part_ref, out_ref, terms_ref, total_ref, sent1, got1, sent2, got2):
    rows = part_ref.shape[0] // shards
    me = lax.axis_index("row")
    peers = [lax.rem(me + d, shards) for d in range(1, shards)]
    barrier = pltpu.get_barrier_semaphore()
    for peer in peers:
        pl.semaphore_signal(
            barrier, inc=1, device_id={"row": peer}, device_id_type=pl.DeviceIdType.MESH
        )
    pl.semaphore_wait(barrier, shards - 1)

    def span(owner):
        return pl.ds(pl.multiple_of(owner * rows, rows), rows)

    def send(src, dst, sent, got, at, peer):
        copy = pltpu.make_async_remote_copy(
            src_ref=src,
            dst_ref=dst,
            send_sem=sent.at[at],
            recv_sem=got.at[at],
            device_id={"row": peer},
            device_id_type=pl.DeviceIdType.MESH,
        )
        copy.start()
        return copy

    first = [
        send(part_ref.at[span(peer)], terms_ref.at[d], sent1, got1, d, peer)
        for d, peer in enumerate(peers)
    ]
    mine = part_ref[span(me)]
    for d, copy in enumerate(first):
        copy.wait_recv()
        mine = mine + terms_ref[d]
    total_ref[span(me)] = mine
    second = [
        send(total_ref.at[span(me)], total_ref.at[span(me)], sent2, got2, d, peer)
        for d, peer in enumerate(peers)
    ]
    for copy in first:
        copy.wait_send()
    for copy in second:
        copy.wait()
    out_ref[...] = total_ref[...]


def row_sum(part):
    shards = lax.axis_size("row")
    rows, width = part.shape
    if shards == 1 or rows % (8 * shards):
        return lax.psum(part, "row")
    return pl.pallas_call(
        lambda *refs: sum_kernel(shards, *refs),
        out_shape=jax.ShapeDtypeStruct(part.shape, part.dtype),
        in_specs=[pl.BlockSpec(memory_space=pltpu.VMEM)],
        out_specs=pl.BlockSpec(memory_space=pltpu.VMEM),
        scratch_shapes=[
            pltpu.VMEM((shards - 1, rows // shards, width), part.dtype),
            pltpu.VMEM(part.shape, part.dtype),
        ]
        + [pltpu.SemaphoreType.DMA((shards - 1,))] * 4,
        compiler_params=pltpu.CompilerParams(
            collective_id=0, has_side_effects=True, vmem_limit_bytes=8 * 2**20
        ),
        cost_estimate=pl.CostEstimate(
            flops=part.size, bytes_accessed=4 * part.size * 4, transcendentals=0
        ),
    )(part)


def body(features, blocks, block_ptr, block_col, held_out, weight, cotangent):
    shards = lax.axis_size("row")
    my_feat = lax.axis_index("feat")
    rows_dev, width_dev = features.shape
    slot_count = blocks.shape[0]
    block_size = blocks.shape[2]
    block_rows = block_ptr.shape[1] - 1
    peer_cap = (slot_count + shards - 1) // shards
    buffer_len = shards * peer_cap
    bf16, f32 = jnp.bfloat16, jnp.float32

    slots = jnp.arange(slot_count, dtype=jnp.int32)
    live = slots < block_ptr[0, block_rows]
    columns = block_col[0]
    source = jnp.where(live, columns // block_rows, 0)
    local = jnp.where(live, columns % block_rows, 0)
    block_row = jnp.sum(
        (slots[:, None] >= block_ptr[0, 1:block_rows][None, :]).astype(jnp.int32), axis=1
    )
    earlier = (
        (source[:, None] == source[None, :]) & live[None, :] & (slots[None, :] < slots[:, None])
    )
    rank = jnp.sum(earlier.astype(jnp.int32), axis=1)
    position = jnp.where(live, source * peer_cap + rank, -1)
    places = jnp.arange(buffer_len, dtype=jnp.int32)
    match = (places[:, None] == position[None, :]).astype(jnp.int32)
    wanted = jnp.sum(match * (local[None, :] + 1), axis=1) - 1
    slot_at = jnp.sum(match * slots[None, :], axis=1)
    brow_at = jnp.sum(match * block_row[None, :], axis=1)
    asked = lax.all_to_all(wanted, "row", split_axis=0, concat_axis=0, tiled=True)

    full_blocks = lax.all_gather(blocks, "feat", axis=1, tiled=True)
    block_shape = (block_size, width_dev)
    outgoing = local_call(
        pack_kernel,
        (asked,),
        (held_out, features.reshape(block_rows, *block_shape)),
        jax.ShapeDtypeStruct((buffer_len, *block_shape), bf16),
        (pltpu.VMEM((block_rows, *block_shape), bf16),),
    )
    arrived = lax.all_to_all(outgoing, "row", split_axis=0, concat_axis=0, tiled=True)

    cot_piece = lax.all_gather(cotangent, "feat", axis=1, tiled=True)
    weight_piece = lax.all_gather(weight, "feat", axis=1, tiled=True)
    weight_mine = lax.dynamic_slice_in_dim(weight_piece, my_feat * width_dev, width_dev, 0)
    agg_grad = lax.dot_general(
        cot_piece, weight_mine, (((1,), (1,)), ((), ())), preferred_element_type=f32
    ).astype(bf16)
    sending = local_call(
        contribution_kernel,
        (slot_at, brow_at),
        (full_blocks, agg_grad.reshape(block_rows, *block_shape)),
        jax.ShapeDtypeStruct((buffer_len, *block_shape), bf16),
        flops=2 * buffer_len * block_size * block_size * width_dev,
    )
    returned = lax.all_to_all(sending, "row", split_axis=0, concat_axis=0, tiled=True)

    aggregated = local_call(
        forward_kernel,
        (jnp.maximum(position, 0), jnp.where(live, block_row, block_rows)),
        (full_blocks, arrived),
        jax.ShapeDtypeStruct((block_rows, *block_shape), bf16),
        (pltpu.VMEM((block_rows + 1, *block_shape), f32),),
        flops=2 * slot_count * block_size * block_size * width_dev,
    ).reshape(rows_dev, width_dev)
    piece = lax.all_gather(aggregated, "feat", axis=1, tiled=True)
    layer_out = jnp.dot(piece, weight, preferred_element_type=f32).astype(bf16)
    grad_part = lax.dot_general(
        piece, cotangent, (((0,), (0,)), ((), ())), preferred_element_type=f32
    )
    grad_total = row_sum(grad_part)
    returned, grad_total, layer_out = lax.optimization_barrier((returned, grad_total, layer_out))
    weight_grad = grad_total * (1.0 / jnp.sqrt(f32(rows_dev * shards)))
    feature_grad = local_call(
        collect_kernel,
        (asked,),
        (held_out, returned),
        jax.ShapeDtypeStruct((block_rows, *block_shape), bf16),
        (pltpu.VMEM((block_rows + 1, *block_shape), f32),),
    ).reshape(rows_dev, width_dev)
    return (layer_out, feature_grad, weight_grad)


def solution(mesh):
    in_specs = (
        P("row", "feat"),
        P("row", "feat", None),
        P("row", None),
        P("row", None),
        P("row", None),
        P(None, "feat"),
        P("row", "feat"),
    )
    out_specs = (P("row", "feat"), P("row", "feat"), P(None, "feat"))
    return jax.shard_map(body, mesh=mesh, in_specs=in_specs, out_specs=out_specs, check_vma=False)
```

```python
import jax
import jax.numpy as jnp
from jax import lax
from jax.experimental import pallas as pl
from jax.experimental.pallas import tpu as pltpu
from jax.sharding import PartitionSpec as P

VMEM_LIMIT = 40 * 2**20


def local_call(kernel, scalars, operands, out_shape, scratch=(), flops=0):
    moved = sum(o.size * o.dtype.itemsize for o in operands)
    moved += out_shape.size * out_shape.dtype.itemsize
    return pl.pallas_call(
        kernel,
        out_shape=out_shape,
        grid_spec=pltpu.PrefetchScalarGridSpec(
            num_scalar_prefetch=len(scalars),
            grid=(),
            in_specs=[pl.BlockSpec(memory_space=pltpu.VMEM)] * len(operands),
            out_specs=pl.BlockSpec(memory_space=pltpu.VMEM),
            scratch_shapes=list(scratch),
        ),
        compiler_params=pltpu.CompilerParams(vmem_limit_bytes=VMEM_LIMIT),
        cost_estimate=pl.CostEstimate(flops=flops, bytes_accessed=moved, transcendentals=0),
    )(*scalars, *operands)


def held_rows(held_ref, b, block_size):
    held = held_ref[...]
    ids = b * block_size + lax.broadcasted_iota(jnp.int32, (block_size, held.shape[1]), 0)
    return jnp.max((ids == held).astype(jnp.float32), axis=1, keepdims=True) > 0.5


def pack_kernel(asked_ref, held_ref, features_ref, out_ref, kept_ref):
    block_rows, block_size, _ = features_ref.shape

    def keep(b, carry):
        rows = features_ref[b].astype(jnp.float32)
        hit = held_rows(held_ref, b, block_size)
        kept_ref[b] = jnp.where(hit, 0.0, rows).astype(kept_ref.dtype)
        return carry

    lax.fori_loop(0, block_rows, keep, 0, unroll=4)

    def copy(p, carry):
        out_ref[p] = kept_ref[jnp.maximum(asked_ref[p], 0)]
        return carry

    lax.fori_loop(0, out_ref.shape[0], copy, 0, unroll=8)


def forward_kernel(position_ref, brow_ref, blocks_ref, arrived_ref, out_ref, acc_ref):
    slot_count = blocks_ref.shape[0]
    acc_ref[...] = jnp.zeros_like(acc_ref)

    def step(g, carry):
        slots = [g * UNROLL + i for i in range(UNROLL)]
        parts = [
            jnp.dot(blocks_ref[k], arrived_ref[position_ref[k]], preferred_element_type=jnp.float32)
            for k in slots
        ]
        for k, part in zip(slots, parts):
            acc_ref[brow_ref[k]] += part
        return carry

    lax.fori_loop(0, slot_count // UNROLL, step, 0)
    for k in range(slot_count // UNROLL * UNROLL, slot_count):
        acc_ref[brow_ref[k]] += jnp.dot(
            blocks_ref[k], arrived_ref[position_ref[k]], preferred_element_type=jnp.float32
        )

    def emit(b, carry):
        out_ref[b] = acc_ref[b].astype(out_ref.dtype)
        return carry

    lax.fori_loop(0, out_ref.shape[0], emit, 0, unroll=4)


UNROLL = 8


def contribution_kernel(slot_ref, brow_ref, blocks_ref, grad_ref, out_ref):
    def one(p):
        out_ref[p] = lax.dot_general(
            blocks_ref[slot_ref[p]],
            grad_ref[brow_ref[p]],
            (((0,), (0,)), ((), ())),
            preferred_element_type=jnp.float32,
        ).astype(out_ref.dtype)

    def step(p, carry):
        one(p)
        return carry

    lax.fori_loop(0, out_ref.shape[0], step, 0, unroll=8)


def collect_kernel(asked_ref, held_ref, returned_ref, out_ref, acc_ref):
    block_rows, block_size, _ = out_ref.shape
    acc_ref[...] = jnp.zeros_like(acc_ref)

    def add(p, carry):
        to = jnp.where(asked_ref[p] < 0, block_rows, asked_ref[p])
        acc_ref[to] += returned_ref[p].astype(jnp.float32)
        return carry

    lax.fori_loop(0, returned_ref.shape[0], add, 0, unroll=8)

    def emit(b, carry):
        hit = held_rows(held_ref, b, block_size)
        out_ref[b] = jnp.where(hit, 0.0, acc_ref[b]).astype(out_ref.dtype)
        return carry

    lax.fori_loop(0, block_rows, emit, 0, unroll=4)


def sum_kernel(shards, part_ref, out_ref, terms_ref, total_ref, sent1, got1, sent2, got2):
    rows = part_ref.shape[0] // shards
    me = lax.axis_index("row")
    peers = [lax.rem(me + d, shards) for d in range(1, shards)]
    barrier = pltpu.get_barrier_semaphore()
    for peer in peers:
        pl.semaphore_signal(
            barrier, inc=1, device_id={"row": peer}, device_id_type=pl.DeviceIdType.MESH
        )
    pl.semaphore_wait(barrier, shards - 1)

    def span(owner):
        return pl.ds(pl.multiple_of(owner * rows, rows), rows)

    def send(src, dst, sent, got, at, peer):
        copy = pltpu.make_async_remote_copy(
            src_ref=src,
            dst_ref=dst,
            send_sem=sent.at[at],
            recv_sem=got.at[at],
            device_id={"row": peer},
            device_id_type=pl.DeviceIdType.MESH,
        )
        copy.start()
        return copy

    first = [
        send(part_ref.at[span(peer)], terms_ref.at[d], sent1, got1, d, peer)
        for d, peer in enumerate(peers)
    ]
    mine = part_ref[span(me)]
    for d, copy in enumerate(first):
        copy.wait_recv()
        mine = mine + terms_ref[d]
    total_ref[span(me)] = mine
    second = [
        send(total_ref.at[span(me)], total_ref.at[span(me)], sent2, got2, d, peer)
        for d, peer in enumerate(peers)
    ]
    for copy in first:
        copy.wait_send()
    for copy in second:
        copy.wait()
    out_ref[...] = total_ref[...]


def row_sum(part):
    shards = lax.axis_size("row")
    rows, width = part.shape
    if shards == 1 or rows % (8 * shards):
        return lax.psum(part, "row")
    return pl.pallas_call(
        lambda *refs: sum_kernel(shards, *refs),
        out_shape=jax.ShapeDtypeStruct(part.shape, part.dtype),
        in_specs=[pl.BlockSpec(memory_space=pltpu.VMEM)],
        out_specs=pl.BlockSpec(memory_space=pltpu.VMEM),
        scratch_shapes=[
            pltpu.VMEM((shards - 1, rows // shards, width), part.dtype),
            pltpu.VMEM(part.shape, part.dtype),
        ]
        + [pltpu.SemaphoreType.DMA((shards - 1,))] * 4,
        compiler_params=pltpu.CompilerParams(
            collective_id=0, has_side_effects=True, vmem_limit_bytes=8 * 2**20
        ),
        cost_estimate=pl.CostEstimate(
            flops=part.size, bytes_accessed=4 * part.size * 4, transcendentals=0
        ),
    )(part)


def gather_kernel(
    shards, meta_ref, held_ref, features_ref, out_ref, all_meta_ref,
    kept_ref, meta_in_ref, own_sem, meta_sent, meta_got, line_sent, line_got, pair_sent, pair_got,
):
    block_rows, block_size, _ = features_ref.shape
    places = shards // 2
    me = lax.axis_index("row")
    at, side = me // 2, lax.rem(me, 2)
    other = 2 * at + 1 - side
    late = max(1, block_rows // 7)
    early = block_rows - late
    cuts = [early * i // 3 for i in range(4)]
    ranges = [pl.ds(a, b - a) for a, b in zip(cuts, cuts[1:])] + [pl.ds(early, late)]
    last = len(ranges) - 1
    streams = [(i, False) for i in range(len(ranges))] + [(last, True)]

    barrier = pltpu.get_barrier_semaphore()
    peers = [lax.rem(me + d, shards) for d in range(1, shards)]
    for peer in peers:
        pl.semaphore_signal(
            barrier, inc=1, device_id={"row": peer}, device_id_type=pl.DeviceIdType.MESH
        )

    def keep(b, carry):
        rows = features_ref[b].astype(jnp.float32)
        hit = held_rows(held_ref, b, block_size)
        kept_ref[b] = jnp.where(hit, 0.0, rows).astype(kept_ref.dtype)
        return carry

    lax.fori_loop(0, block_rows, keep, 0, unroll=4)
    own = pltpu.make_async_copy(kept_ref, out_ref.at[me], own_sem)
    own.start()
    pl.semaphore_wait(barrier, shards - 1)

    def remote(src, dst, sent, got, peer):
        return pltpu.make_async_remote_copy(
            src_ref=src,
            dst_ref=dst,
            send_sem=sent,
            recv_sem=got,
            device_id={"row": peer},
            device_id_type=pl.DeviceIdType.MESH,
        )

    def piece(origin, part):
        return out_ref.at[origin, ranges[part]]

    def along(way, hop, n, origin_at):
        part, crossed = streams[n]
        origin = 2 * origin_at + (1 - side if crossed else side)
        src = kept_ref.at[ranges[part]] if hop == 1 and not crossed else piece(origin, part)
        k = (0 if way > 0 else 1, hop - 1, n)
        return remote(src, piece(origin, part), line_sent.at[k], line_got.at[k], me + 2 * way)

    def across(way, hop, part, origin_at):
        origin = 2 * origin_at + side
        src = kept_ref.at[ranges[part]] if hop == 0 else piece(origin, part)
        k = (0 if way > 0 else 1, hop, part)
        return remote(src, piece(origin, part), pair_sent.at[k], pair_got.at[k], other)

    def ahead(way, hops=1):
        return (at + way * hops >= 0) & (at + way * hops < places)

    def start_line(way, n):
        @pl.when(ahead(way))
        def _():
            along(way, 1, n, at).start()

    order = [last] + list(range(last))
    for part in order:
        across(1, 0, part, at).start()
        for way in (1, -1):
            start_line(way, part)
    metas = [
        remote(meta_ref, meta_in_ref.at[me], meta_sent.at[d], meta_got.at[d], peer)
        for d, peer in enumerate(peers)
    ]
    for copy in metas:
        copy.start()
    across(1, 0, last, at).wait_recv()
    for way in (1, -1):
        start_line(way, len(streams) - 1)

    walk = [last] + list(range(last)) + [len(streams) - 1]
    for hop in range(1, places):
        for n in walk:
            part, crossed = streams[n]
            for way in (1, -1):

                @pl.when(ahead(-way, hop))
                def _():
                    along(way, hop, n, at - way * hop).wait_recv()
                    if part != last:
                        across(way, hop, part, at - way * hop).start()
                    if hop < places - 1:

                        @pl.when(ahead(way))
                        def _():
                            along(way, hop + 1, n, at - way * hop).start()

    for part in range(last):
        across(1, 0, part, at).wait_recv()
    for part in range(last + 1):
        across(1, 0, part, at).wait_send()
    for way in (1, -1):
        for n in range(len(streams)):

            @pl.when(ahead(way))
            def _():
                along(way, 1, n, at).wait_send()

    for hop in range(1, places):
        for way in (1, -1):

            @pl.when(ahead(-way, hop))
            def _():
                for part in range(last):
                    across(way, hop, part, at - way * hop).wait()
                if hop < places - 1:

                    @pl.when(ahead(way))
                    def _():
                        for n in range(len(streams)):
                            along(way, hop + 1, n, at - way * hop).wait_send()

    for copy in metas:
        copy.wait()
    own.wait()
    all_meta_ref[...] = meta_in_ref[...]
    all_meta_ref[me] = meta_ref[...]


def gather_kept(meta, held_out, features, shards):
    block_rows, block_size, width = features.shape
    streams, places = 5, shards // 2
    return pl.pallas_call(
        lambda *refs: gather_kernel(shards, *refs),
        out_shape=(
            jax.ShapeDtypeStruct((shards, *features.shape), features.dtype),
            jax.ShapeDtypeStruct((shards, *meta.shape), meta.dtype),
        ),
        in_specs=[pl.BlockSpec(memory_space=pltpu.VMEM)] * 3,
        out_specs=(
            pl.BlockSpec(memory_space=pl.ANY),
            pl.BlockSpec(memory_space=pltpu.VMEM),
        ),
        scratch_shapes=[
            pltpu.VMEM(features.shape, features.dtype),
            pltpu.VMEM((shards, *meta.shape), meta.dtype),
            pltpu.SemaphoreType.DMA,
            pltpu.SemaphoreType.DMA((shards - 1,)),
            pltpu.SemaphoreType.DMA((shards - 1,)),
            pltpu.SemaphoreType.DMA((2, places, streams)),
            pltpu.SemaphoreType.DMA((2, places, streams)),
            pltpu.SemaphoreType.DMA((2, places, streams)),
            pltpu.SemaphoreType.DMA((2, places, streams)),
        ],
        compiler_params=pltpu.CompilerParams(
            collective_id=1, has_side_effects=True, vmem_limit_bytes=VMEM_LIMIT
        ),
        cost_estimate=pl.CostEstimate(
            flops=0, bytes_accessed=30 * shards * features.size, transcendentals=0
        ),
    )(meta, held_out, features)


def lane_pad(x):
    return jnp.pad(x, ((0, 0), (0, -x.shape[1] % 128)))


def body(features, blocks, block_ptr, block_col, held_out, weight, cotangent):
    shards = lax.axis_size("row")
    my_feat = lax.axis_index("feat")
    rows_dev, width_dev = features.shape
    slot_count = blocks.shape[0]
    block_size = blocks.shape[2]
    block_rows = block_ptr.shape[1] - 1
    peer_cap = (slot_count + shards - 1) // shards
    buffer_len = shards * peer_cap
    bf16, f32 = jnp.bfloat16, jnp.float32

    slots = jnp.arange(slot_count, dtype=jnp.int32)
    live = slots < block_ptr[0, block_rows]
    columns = block_col[0]
    source = jnp.where(live, columns // block_rows, 0)
    local = jnp.where(live, columns % block_rows, 0)
    block_row = jnp.sum(
        (slots[:, None] >= block_ptr[0, 1:block_rows][None, :]).astype(jnp.int32), axis=1
    )
    earlier = (
        (source[:, None] == source[None, :]) & live[None, :] & (slots[None, :] < slots[:, None])
    )
    rank = jnp.sum(earlier.astype(jnp.int32), axis=1)
    position = jnp.where(live, source * peer_cap + rank, -1)
    places = jnp.arange(buffer_len, dtype=jnp.int32)
    match = (places[:, None] == position[None, :]).astype(jnp.int32)
    wanted = jnp.sum(match * (local[None, :] + 1), axis=1) - 1
    slot_at = jnp.sum(match * slots[None, :], axis=1)
    brow_at = jnp.sum(match * block_row[None, :], axis=1)

    block_shape = (block_size, width_dev)
    feature_blocks = features.reshape(block_rows, *block_shape)
    held = held_out
    dense = jnp.concatenate([cotangent, weight], axis=0)
    dense_piece = lax.all_gather(dense, "feat", axis=1, tiled=True)
    full_blocks = lax.all_gather(blocks, "feat", axis=1, tiled=True)
    whole = shards > 2 and shards % 2 == 0 and block_rows <= 2 * peer_cap
    if whole:
        span = max(block_rows + 1, slot_count)
        tables = jnp.concatenate(
            [
                jnp.pad(block_ptr, ((0, 0), (0, span - block_rows - 1))),
                jnp.pad(block_col, ((0, 0), (0, span - slot_count))),
            ],
            axis=0,
        )
        meta = lane_pad(jnp.pad(tables, ((0, 6), (0, 0))))
        gathered, all_meta = gather_kept(meta, held, feature_blocks, shards)
        gathered, dense_piece, full_blocks = lax.optimization_barrier(
            (gathered, dense_piece, full_blocks)
        )
        me = lax.axis_index("row")
        all_col = all_meta[:, 1, :slot_count]
        all_live = slots[None, :] < all_meta[:, 0, block_rows][:, None]
        named = all_live & (all_col // block_rows == me)
        ahead = (slots[:, None] < slots[None, :]).astype(f32)
        order = jnp.dot(named.astype(f32), ahead, preferred_element_type=f32).astype(jnp.int32)
        at_rank = named[:, None, :] & (
            order[:, None, :] == jnp.arange(peer_cap, dtype=jnp.int32)[None, :, None]
        )
        asked = jnp.sum(
            jnp.where(at_rank, all_col[:, None, :] % block_rows + 1, 0), axis=2
        ).reshape(buffer_len) - 1
        arrived = gathered.reshape(shards * block_rows, *block_shape)
        found = jnp.where(live, columns, 0)
    else:
        asked = lax.all_to_all(wanted, "row", split_axis=0, concat_axis=0, tiled=True)
        outgoing = local_call(
            pack_kernel,
            (asked,),
            (held, feature_blocks),
            jax.ShapeDtypeStruct((buffer_len, *block_shape), bf16),
            (pltpu.VMEM((block_rows, *block_shape), bf16),),
        )
        arrived = lax.all_to_all(outgoing, "row", split_axis=0, concat_axis=0, tiled=True)
        found = jnp.maximum(position, 0)
    cot_piece, weight_piece = dense_piece[:rows_dev], dense_piece[rows_dev:]
    weight_mine = lax.dynamic_slice_in_dim(weight_piece, my_feat * width_dev, width_dev, 0)
    agg_grad = lax.dot_general(
        cot_piece, weight_mine, (((1,), (1,)), ((), ())), preferred_element_type=f32
    ).astype(bf16)
    sending = local_call(
        contribution_kernel,
        (slot_at, brow_at),
        (full_blocks, agg_grad.reshape(block_rows, *block_shape)),
        jax.ShapeDtypeStruct((buffer_len, *block_shape), bf16),
        flops=2 * buffer_len * block_size * block_size * width_dev,
    )
    returned = lax.all_to_all(sending, "row", split_axis=0, concat_axis=0, tiled=True)

    aggregated = local_call(
        forward_kernel,
        (found, jnp.where(live, block_row, block_rows)),
        (full_blocks, arrived),
        jax.ShapeDtypeStruct((block_rows, *block_shape), bf16),
        (pltpu.VMEM((block_rows + 1, *block_shape), f32),),
        flops=2 * slot_count * block_size * block_size * width_dev,
    ).reshape(rows_dev, width_dev)
    piece = lax.all_gather(aggregated, "feat", axis=1, tiled=True)
    layer_out = jnp.dot(piece, weight, preferred_element_type=f32).astype(bf16)
    grad_part = lax.dot_general(
        piece, cotangent, (((0,), (0,)), ((), ())), preferred_element_type=f32
    )
    grad_total = row_sum(grad_part)
    returned, grad_total, layer_out = lax.optimization_barrier((returned, grad_total, layer_out))
    weight_grad = grad_total * (1.0 / jnp.sqrt(f32(rows_dev * shards)))
    feature_grad = local_call(
        collect_kernel,
        (asked,),
        (held, returned),
        jax.ShapeDtypeStruct((block_rows, *block_shape), bf16),
        (pltpu.VMEM((block_rows + 1, *block_shape), f32),),
    ).reshape(rows_dev, width_dev)
    return (layer_out, feature_grad, weight_grad)


def solution(mesh):
    in_specs = (
        P("row", "feat"),
        P("row", "feat", None),
        P("row", None),
        P("row", None),
        P("row", None),
        P(None, "feat"),
        P("row", "feat"),
    )
    out_specs = (P("row", "feat"), P("row", "feat"), P(None, "feat"))
    return jax.shard_map(body, mesh=mesh, in_specs=in_specs, out_specs=out_specs, check_vma=False)
```

```python
import jax
import jax.numpy as jnp
from jax import lax
from jax.experimental import pallas as pl
from jax.experimental.pallas import tpu as pltpu
from jax.sharding import PartitionSpec as P

VMEM_LIMIT = 58 * 2**20


def local_call(kernel, scalars, operands, out_shape, scratch=(), flops=0):
    moved = sum(o.size * o.dtype.itemsize for o in operands)
    moved += out_shape.size * out_shape.dtype.itemsize
    return pl.pallas_call(
        kernel,
        out_shape=out_shape,
        grid_spec=pltpu.PrefetchScalarGridSpec(
            num_scalar_prefetch=len(scalars),
            grid=(),
            in_specs=[pl.BlockSpec(memory_space=pltpu.VMEM)] * len(operands),
            out_specs=pl.BlockSpec(memory_space=pltpu.VMEM),
            scratch_shapes=list(scratch),
        ),
        compiler_params=pltpu.CompilerParams(vmem_limit_bytes=VMEM_LIMIT),
        cost_estimate=pl.CostEstimate(flops=flops, bytes_accessed=moved, transcendentals=0),
    )(*scalars, *operands)


def held_rows(held_ref, b, block_size):
    held = held_ref[...]
    ids = b * block_size + lax.broadcasted_iota(jnp.int32, (block_size, held.shape[1]), 0)
    return jnp.max((ids == held).astype(jnp.float32), axis=1, keepdims=True) > 0.5


def pack_kernel(asked_ref, held_ref, features_ref, out_ref, kept_ref):
    block_rows, block_size, _ = features_ref.shape

    def keep(b, carry):
        rows = features_ref[b].astype(jnp.float32)
        hit = held_rows(held_ref, b, block_size)
        kept_ref[b] = jnp.where(hit, 0.0, rows).astype(kept_ref.dtype)
        return carry

    lax.fori_loop(0, block_rows, keep, 0, unroll=4)

    def copy(p, carry):
        out_ref[p] = kept_ref[jnp.maximum(asked_ref[p], 0)]
        return carry

    lax.fori_loop(0, out_ref.shape[0], copy, 0, unroll=8)


def forward_kernel(position_ref, brow_ref, blocks_ref, arrived_ref, out_ref, acc_ref):
    slot_count = blocks_ref.shape[0]
    acc_ref[...] = jnp.zeros_like(acc_ref)

    def step(g, carry):
        slots = [g * UNROLL + i for i in range(UNROLL)]
        parts = [
            jnp.dot(blocks_ref[k], arrived_ref[position_ref[k]], preferred_element_type=jnp.float32)
            for k in slots
        ]
        for k, part in zip(slots, parts):
            acc_ref[brow_ref[k]] += part
        return carry

    lax.fori_loop(0, slot_count // UNROLL, step, 0)
    for k in range(slot_count // UNROLL * UNROLL, slot_count):
        acc_ref[brow_ref[k]] += jnp.dot(
            blocks_ref[k], arrived_ref[position_ref[k]], preferred_element_type=jnp.float32
        )

    def emit(b, carry):
        out_ref[b] = acc_ref[b].astype(out_ref.dtype)
        return carry

    lax.fori_loop(0, out_ref.shape[0], emit, 0, unroll=4)


UNROLL = 8


def contribution_kernel(slot_ref, brow_ref, blocks_ref, grad_ref, out_ref):
    def one(p):
        out_ref[p] = lax.dot_general(
            blocks_ref[slot_ref[p]],
            grad_ref[brow_ref[p]],
            (((0,), (0,)), ((), ())),
            preferred_element_type=jnp.float32,
        ).astype(out_ref.dtype)

    def step(p, carry):
        one(p)
        return carry

    lax.fori_loop(0, out_ref.shape[0], step, 0, unroll=8)


def collect_kernel(asked_ref, held_ref, returned_ref, out_ref, acc_ref):
    block_rows, block_size, _ = out_ref.shape
    acc_ref[...] = jnp.zeros_like(acc_ref)

    def add(p, carry):
        to = jnp.where(asked_ref[p] < 0, block_rows, asked_ref[p])
        acc_ref[to] += returned_ref[p].astype(jnp.float32)
        return carry

    lax.fori_loop(0, returned_ref.shape[0], add, 0, unroll=8)

    def emit(b, carry):
        hit = held_rows(held_ref, b, block_size)
        out_ref[b] = jnp.where(hit, 0.0, acc_ref[b]).astype(out_ref.dtype)
        return carry

    lax.fori_loop(0, block_rows, emit, 0, unroll=4)


def sum_kernel(shards, part_ref, out_ref, terms_ref, total_ref, sent1, got1, sent2, got2):
    rows = part_ref.shape[0] // shards
    me = lax.axis_index("row")
    peers = [lax.rem(me + d, shards) for d in range(1, shards)]
    barrier = pltpu.get_barrier_semaphore()
    for peer in peers:
        pl.semaphore_signal(
            barrier, inc=1, device_id={"row": peer}, device_id_type=pl.DeviceIdType.MESH
        )
    pl.semaphore_wait(barrier, shards - 1)

    def span(owner):
        return pl.ds(pl.multiple_of(owner * rows, rows), rows)

    def send(src, dst, sent, got, at, peer):
        copy = pltpu.make_async_remote_copy(
            src_ref=src,
            dst_ref=dst,
            send_sem=sent.at[at],
            recv_sem=got.at[at],
            device_id={"row": peer},
            device_id_type=pl.DeviceIdType.MESH,
        )
        copy.start()
        return copy

    first = [
        send(part_ref.at[span(peer)], terms_ref.at[d], sent1, got1, d, peer)
        for d, peer in enumerate(peers)
    ]
    mine = part_ref[span(me)]
    for d, copy in enumerate(first):
        copy.wait_recv()
        mine = mine + terms_ref[d]
    total_ref[span(me)] = mine
    second = [
        send(total_ref.at[span(me)], total_ref.at[span(me)], sent2, got2, d, peer)
        for d, peer in enumerate(peers)
    ]
    for copy in first:
        copy.wait_send()
    for copy in second:
        copy.wait()
    out_ref[...] = total_ref[...]


def row_sum(part):
    shards = lax.axis_size("row")
    rows, width = part.shape
    if shards == 1 or rows % (8 * shards):
        return lax.psum(part, "row")
    return pl.pallas_call(
        lambda *refs: sum_kernel(shards, *refs),
        out_shape=jax.ShapeDtypeStruct(part.shape, part.dtype),
        in_specs=[pl.BlockSpec(memory_space=pltpu.VMEM)],
        out_specs=pl.BlockSpec(memory_space=pltpu.VMEM),
        scratch_shapes=[
            pltpu.VMEM((shards - 1, rows // shards, width), part.dtype),
            pltpu.VMEM(part.shape, part.dtype),
        ]
        + [pltpu.SemaphoreType.DMA((shards - 1,))] * 4,
        compiler_params=pltpu.CompilerParams(
            collective_id=0, has_side_effects=True, vmem_limit_bytes=8 * 2**20
        ),
        cost_estimate=pl.CostEstimate(
            flops=part.size, bytes_accessed=4 * part.size * 4, transcendentals=0
        ),
    )(part)


def gather_kernel(
    shards, meta_ref, held_ref, features_ref, out_ref, all_meta_ref,
    kept_ref, meta_in_ref, own_sem, meta_sent, meta_got, line_sent, line_got, pair_sent, pair_got,
):
    block_rows, block_size, _ = features_ref.shape
    places = shards // 2
    me = lax.axis_index("row")
    at, side = me // 2, lax.rem(me, 2)
    other = 2 * at + 1 - side
    late = max(1, block_rows // 7)
    early = block_rows - late
    cuts = [early * i // 3 for i in range(4)]
    ranges = [pl.ds(a, b - a) for a, b in zip(cuts, cuts[1:])] + [pl.ds(early, late)]
    last = len(ranges) - 1
    streams = [(i, False) for i in range(len(ranges))] + [(last, True)]

    barrier = pltpu.get_barrier_semaphore()
    peers = [lax.rem(me + d, shards) for d in range(1, shards)]
    for peer in peers:
        pl.semaphore_signal(
            barrier, inc=1, device_id={"row": peer}, device_id_type=pl.DeviceIdType.MESH
        )

    def keep(b, carry):
        rows = features_ref[b].astype(jnp.float32)
        hit = held_rows(held_ref, b, block_size)
        kept_ref[b] = jnp.where(hit, 0.0, rows).astype(kept_ref.dtype)
        return carry

    lax.fori_loop(0, block_rows, keep, 0, unroll=4)
    own = pltpu.make_async_copy(kept_ref, out_ref.at[me], own_sem)
    own.start()
    pl.semaphore_wait(barrier, shards - 1)

    def remote(src, dst, sent, got, peer):
        return pltpu.make_async_remote_copy(
            src_ref=src,
            dst_ref=dst,
            send_sem=sent,
            recv_sem=got,
            device_id={"row": peer},
            device_id_type=pl.DeviceIdType.MESH,
        )

    def piece(origin, part):
        return out_ref.at[origin, ranges[part]]

    def along(way, hop, n, origin_at):
        part, crossed = streams[n]
        origin = 2 * origin_at + (1 - side if crossed else side)
        src = kept_ref.at[ranges[part]] if hop == 1 and not crossed else piece(origin, part)
        k = (0 if way > 0 else 1, hop - 1, n)
        return remote(src, piece(origin, part), line_sent.at[k], line_got.at[k], me + 2 * way)

    def across(way, hop, part, origin_at):
        origin = 2 * origin_at + side
        src = kept_ref.at[ranges[part]] if hop == 0 else piece(origin, part)
        k = (0 if way > 0 else 1, hop, part)
        return remote(src, piece(origin, part), pair_sent.at[k], pair_got.at[k], other)

    def ahead(way, hops=1):
        return (at + way * hops >= 0) & (at + way * hops < places)

    def start_line(way, n):
        @pl.when(ahead(way))
        def _():
            along(way, 1, n, at).start()

    order = [last] + list(range(last))
    for part in order:
        across(1, 0, part, at).start()
        for way in (1, -1):
            start_line(way, part)
    metas = [
        remote(meta_ref, meta_in_ref.at[me], meta_sent.at[d], meta_got.at[d], peer)
        for d, peer in enumerate(peers)
    ]
    for copy in metas:
        copy.start()
    across(1, 0, last, at).wait_recv()
    for way in (1, -1):
        start_line(way, len(streams) - 1)

    walk = [last] + list(range(last)) + [len(streams) - 1]
    for hop in range(1, places):
        for n in walk:
            part, crossed = streams[n]
            for way in (1, -1):

                @pl.when(ahead(-way, hop))
                def _():
                    along(way, hop, n, at - way * hop).wait_recv()
                    if part != last:
                        across(way, hop, part, at - way * hop).start()
                    if hop < places - 1:

                        @pl.when(ahead(way))
                        def _():
                            along(way, hop + 1, n, at - way * hop).start()

    for part in range(last):
        across(1, 0, part, at).wait_recv()
    for part in range(last + 1):
        across(1, 0, part, at).wait_send()
    for way in (1, -1):
        for n in range(len(streams)):

            @pl.when(ahead(way))
            def _():
                along(way, 1, n, at).wait_send()

    for hop in range(1, places):
        for way in (1, -1):

            @pl.when(ahead(-way, hop))
            def _():
                for part in range(last):
                    across(way, hop, part, at - way * hop).wait()
                if hop < places - 1:

                    @pl.when(ahead(way))
                    def _():
                        for n in range(len(streams)):
                            along(way, hop + 1, n, at - way * hop).wait_send()

    for copy in metas:
        copy.wait()
    own.wait()
    all_meta_ref[...] = meta_in_ref[...]
    all_meta_ref[me] = meta_ref[...]


def gather_kept(meta, held_out, features, shards):
    block_rows, block_size, width = features.shape
    streams, places = 5, shards // 2
    return pl.pallas_call(
        lambda *refs: gather_kernel(shards, *refs),
        out_shape=(
            jax.ShapeDtypeStruct((shards, *features.shape), features.dtype),
            jax.ShapeDtypeStruct((shards, *meta.shape), meta.dtype),
        ),
        in_specs=[pl.BlockSpec(memory_space=pltpu.VMEM)] * 3,
        out_specs=(
            pl.BlockSpec(memory_space=pl.ANY),
            pl.BlockSpec(memory_space=pltpu.VMEM),
        ),
        scratch_shapes=[
            pltpu.VMEM(features.shape, features.dtype),
            pltpu.VMEM((shards, *meta.shape), meta.dtype),
            pltpu.SemaphoreType.DMA,
            pltpu.SemaphoreType.DMA((shards - 1,)),
            pltpu.SemaphoreType.DMA((shards - 1,)),
            pltpu.SemaphoreType.DMA((2, places, streams)),
            pltpu.SemaphoreType.DMA((2, places, streams)),
            pltpu.SemaphoreType.DMA((2, places, streams)),
            pltpu.SemaphoreType.DMA((2, places, streams)),
        ],
        compiler_params=pltpu.CompilerParams(
            collective_id=1, has_side_effects=True, vmem_limit_bytes=VMEM_LIMIT
        ),
        cost_estimate=pl.CostEstimate(
            flops=0, bytes_accessed=30 * shards * features.size, transcendentals=0
        ),
    )(meta, held_out, features)


def lane_pad(x):
    return jnp.pad(x, ((0, 0), (0, -x.shape[1] % 128)))


def body(features, blocks, block_ptr, block_col, held_out, weight, cotangent):
    shards = lax.axis_size("row")
    my_feat = lax.axis_index("feat")
    rows_dev, width_dev = features.shape
    slot_count = blocks.shape[0]
    block_size = blocks.shape[2]
    block_rows = block_ptr.shape[1] - 1
    peer_cap = (slot_count + shards - 1) // shards
    buffer_len = shards * peer_cap
    bf16, f32 = jnp.bfloat16, jnp.float32

    slots = jnp.arange(slot_count, dtype=jnp.int32)
    live = slots < block_ptr[0, block_rows]
    columns = block_col[0]
    source = jnp.where(live, columns // block_rows, 0)
    local = jnp.where(live, columns % block_rows, 0)
    block_row = jnp.sum(
        (slots[:, None] >= block_ptr[0, 1:block_rows][None, :]).astype(jnp.int32), axis=1
    )
    earlier = (
        (source[:, None] == source[None, :]) & live[None, :] & (slots[None, :] < slots[:, None])
    )
    rank = jnp.sum(earlier.astype(jnp.int32), axis=1)
    position = jnp.where(live, source * peer_cap + rank, -1)
    places = jnp.arange(buffer_len, dtype=jnp.int32)
    match = (places[:, None] == position[None, :]).astype(jnp.int32)
    wanted = jnp.sum(match * (local[None, :] + 1), axis=1) - 1
    slot_at = jnp.sum(match * slots[None, :], axis=1)
    brow_at = jnp.sum(match * block_row[None, :], axis=1)

    block_shape = (block_size, width_dev)
    feature_blocks = features.reshape(block_rows, *block_shape)
    held = held_out
    dense = jnp.concatenate([cotangent, weight], axis=0)
    dense_piece = lax.all_gather(dense, "feat", axis=1, tiled=True)
    full_blocks = lax.all_gather(blocks, "feat", axis=1, tiled=True)
    whole = shards > 2 and shards % 2 == 0 and block_rows <= 2 * peer_cap
    if whole:
        span = max(block_rows + 1, slot_count)
        tables = jnp.concatenate(
            [
                jnp.pad(block_ptr, ((0, 0), (0, span - block_rows - 1))),
                jnp.pad(block_col, ((0, 0), (0, span - slot_count))),
            ],
            axis=0,
        )
        meta = lane_pad(jnp.pad(tables, ((0, 6), (0, 0))))
        gathered, all_meta = gather_kept(meta, held, feature_blocks, shards)
        all_meta, dense_piece, full_blocks = lax.optimization_barrier(
            (all_meta, dense_piece, full_blocks)
        )
        me = lax.axis_index("row")
        all_col = all_meta[:, 1, :slot_count]
        all_live = slots[None, :] < all_meta[:, 0, block_rows][:, None]
        named = all_live & (all_col // block_rows == me)
        ahead = (slots[:, None] < slots[None, :]).astype(f32)
        order = jnp.dot(named.astype(f32), ahead, preferred_element_type=f32).astype(jnp.int32)
        at_rank = named[:, None, :] & (
            order[:, None, :] == jnp.arange(peer_cap, dtype=jnp.int32)[None, :, None]
        )
        asked = jnp.sum(
            jnp.where(at_rank, all_col[:, None, :] % block_rows + 1, 0), axis=2
        ).reshape(buffer_len) - 1
        arrived = gathered.reshape(shards * block_rows, *block_shape)
        found = jnp.where(live, columns, 0)
    else:
        asked = lax.all_to_all(wanted, "row", split_axis=0, concat_axis=0, tiled=True)
        outgoing = local_call(
            pack_kernel,
            (asked,),
            (held, feature_blocks),
            jax.ShapeDtypeStruct((buffer_len, *block_shape), bf16),
            (pltpu.VMEM((block_rows, *block_shape), bf16),),
        )
        arrived = lax.all_to_all(outgoing, "row", split_axis=0, concat_axis=0, tiled=True)
        found = jnp.maximum(position, 0)
    cot_piece, weight_piece = dense_piece[:rows_dev], dense_piece[rows_dev:]
    weight_mine = lax.dynamic_slice_in_dim(weight_piece, my_feat * width_dev, width_dev, 0)
    agg_grad = lax.dot_general(
        cot_piece, weight_mine, (((1,), (1,)), ((), ())), preferred_element_type=f32
    ).astype(bf16)
    sending = local_call(
        contribution_kernel,
        (slot_at, brow_at),
        (full_blocks, agg_grad.reshape(block_rows, *block_shape)),
        jax.ShapeDtypeStruct((buffer_len, *block_shape), bf16),
        flops=2 * buffer_len * block_size * block_size * width_dev,
    )
    returned = lax.all_to_all(sending, "row", split_axis=0, concat_axis=0, tiled=True)

    aggregated = local_call(
        forward_kernel,
        (found, jnp.where(live, block_row, block_rows)),
        (full_blocks, arrived),
        jax.ShapeDtypeStruct((block_rows, *block_shape), bf16),
        (pltpu.VMEM((block_rows + 1, *block_shape), f32),),
        flops=2 * slot_count * block_size * block_size * width_dev,
    ).reshape(rows_dev, width_dev)
    piece = lax.all_gather(aggregated, "feat", axis=1, tiled=True)
    layer_out = jnp.dot(piece, weight, preferred_element_type=f32).astype(bf16)
    grad_part = lax.dot_general(
        piece, cotangent, (((0,), (0,)), ((), ())), preferred_element_type=f32
    )
    grad_part, layer_out = lax.optimization_barrier((grad_part, layer_out))
    grad_total = row_sum(grad_part)
    returned, grad_total = lax.optimization_barrier((returned, grad_total))
    weight_grad = grad_total * (1.0 / jnp.sqrt(f32(rows_dev * shards)))
    feature_grad = local_call(
        collect_kernel,
        (asked,),
        (held, returned),
        jax.ShapeDtypeStruct((block_rows, *block_shape), bf16),
        (pltpu.VMEM((block_rows + 1, *block_shape), f32),),
    ).reshape(rows_dev, width_dev)
    return (layer_out, feature_grad, weight_grad)


def solution(mesh):
    in_specs = (
        P("row", "feat"),
        P("row", "feat", None),
        P("row", None),
        P("row", None),
        P("row", None),
        P(None, "feat"),
        P("row", "feat"),
    )
    out_specs = (P("row", "feat"), P("row", "feat"), P(None, "feat"))
    return jax.shard_map(body, mesh=mesh, in_specs=in_specs, out_specs=out_specs, check_vma=False)
```

```python
import jax
import jax.numpy as jnp
from jax import lax
from jax.experimental import pallas as pl
from jax.experimental.pallas import tpu as pltpu
from jax.sharding import PartitionSpec as P

VMEM_LIMIT = 58 * 2**20


def local_call(kernel, scalars, operands, out_shape, scratch=(), flops=0):
    moved = sum(o.size * o.dtype.itemsize for o in operands)
    moved += out_shape.size * out_shape.dtype.itemsize
    return pl.pallas_call(
        kernel,
        out_shape=out_shape,
        grid_spec=pltpu.PrefetchScalarGridSpec(
            num_scalar_prefetch=len(scalars),
            grid=(),
            in_specs=[pl.BlockSpec(memory_space=pltpu.VMEM)] * len(operands),
            out_specs=pl.BlockSpec(memory_space=pltpu.VMEM),
            scratch_shapes=list(scratch),
        ),
        compiler_params=pltpu.CompilerParams(vmem_limit_bytes=VMEM_LIMIT),
        cost_estimate=pl.CostEstimate(flops=flops, bytes_accessed=moved, transcendentals=0),
    )(*scalars, *operands)


def held_rows(held_ref, b, block_size):
    held = held_ref[...]
    ids = b * block_size + lax.broadcasted_iota(jnp.int32, (block_size, held.shape[1]), 0)
    return jnp.max((ids == held).astype(jnp.float32), axis=1, keepdims=True) > 0.5


def pack_kernel(asked_ref, held_ref, features_ref, out_ref, kept_ref):
    block_rows, block_size, _ = features_ref.shape

    def keep(b, carry):
        rows = features_ref[b].astype(jnp.float32)
        hit = held_rows(held_ref, b, block_size)
        kept_ref[b] = jnp.where(hit, 0.0, rows).astype(kept_ref.dtype)
        return carry

    lax.fori_loop(0, block_rows, keep, 0, unroll=4)

    def copy(p, carry):
        out_ref[p] = kept_ref[jnp.maximum(asked_ref[p], 0)]
        return carry

    lax.fori_loop(0, out_ref.shape[0], copy, 0, unroll=8)


def forward_kernel(position_ref, brow_ref, blocks_ref, arrived_ref, out_ref, acc_ref):
    slot_count = blocks_ref.shape[0]
    acc_ref[...] = jnp.zeros_like(acc_ref)

    def step(g, carry):
        slots = [g * UNROLL + i for i in range(UNROLL)]
        parts = [
            jnp.dot(blocks_ref[k], arrived_ref[position_ref[k]], preferred_element_type=jnp.float32)
            for k in slots
        ]
        for k, part in zip(slots, parts):
            acc_ref[brow_ref[k]] += part
        return carry

    lax.fori_loop(0, slot_count // UNROLL, step, 0)
    for k in range(slot_count // UNROLL * UNROLL, slot_count):
        acc_ref[brow_ref[k]] += jnp.dot(
            blocks_ref[k], arrived_ref[position_ref[k]], preferred_element_type=jnp.float32
        )

    def emit(b, carry):
        out_ref[b] = acc_ref[b].astype(out_ref.dtype)
        return carry

    lax.fori_loop(0, out_ref.shape[0], emit, 0, unroll=4)


UNROLL = 8


def contribution_kernel(slot_ref, brow_ref, blocks_ref, grad_ref, out_ref):
    def one(p):
        out_ref[p] = lax.dot_general(
            blocks_ref[slot_ref[p]],
            grad_ref[brow_ref[p]],
            (((0,), (0,)), ((), ())),
            preferred_element_type=jnp.float32,
        ).astype(out_ref.dtype)

    def step(p, carry):
        one(p)
        return carry

    lax.fori_loop(0, out_ref.shape[0], step, 0, unroll=8)


def collect_kernel(asked_ref, held_ref, returned_ref, out_ref, acc_ref):
    block_rows, block_size, _ = out_ref.shape
    acc_ref[...] = jnp.zeros_like(acc_ref)

    def add(p, carry):
        to = jnp.where(asked_ref[p] < 0, block_rows, asked_ref[p])
        acc_ref[to] += returned_ref[p].astype(jnp.float32)
        return carry

    lax.fori_loop(0, returned_ref.shape[0], add, 0, unroll=8)

    def emit(b, carry):
        hit = held_rows(held_ref, b, block_size)
        out_ref[b] = jnp.where(hit, 0.0, acc_ref[b]).astype(out_ref.dtype)
        return carry

    lax.fori_loop(0, block_rows, emit, 0, unroll=4)


def sum_kernel(shards, part_ref, out_ref, terms_ref, total_ref, sent1, got1, sent2, got2):
    rows = part_ref.shape[0] // shards
    me = lax.axis_index("row")
    peers = [lax.rem(me + d, shards) for d in range(1, shards)]
    barrier = pltpu.get_barrier_semaphore()
    for peer in peers:
        pl.semaphore_signal(
            barrier, inc=1, device_id={"row": peer}, device_id_type=pl.DeviceIdType.MESH
        )
    pl.semaphore_wait(barrier, shards - 1)

    def span(owner):
        return pl.ds(pl.multiple_of(owner * rows, rows), rows)

    def send(src, dst, sent, got, at, peer):
        copy = pltpu.make_async_remote_copy(
            src_ref=src,
            dst_ref=dst,
            send_sem=sent.at[at],
            recv_sem=got.at[at],
            device_id={"row": peer},
            device_id_type=pl.DeviceIdType.MESH,
        )
        copy.start()
        return copy

    first = [
        send(part_ref.at[span(peer)], terms_ref.at[d], sent1, got1, d, peer)
        for d, peer in enumerate(peers)
    ]
    mine = part_ref[span(me)]
    for d, copy in enumerate(first):
        copy.wait_recv()
        mine = mine + terms_ref[d]
    total_ref[span(me)] = mine
    second = [
        send(total_ref.at[span(me)], total_ref.at[span(me)], sent2, got2, d, peer)
        for d, peer in enumerate(peers)
    ]
    for copy in first:
        copy.wait_send()
    for copy in second:
        copy.wait()
    out_ref[...] = total_ref[...]


def row_sum(part):
    shards = lax.axis_size("row")
    rows, width = part.shape
    if shards == 1 or rows % (8 * shards):
        return lax.psum(part, "row")
    return pl.pallas_call(
        lambda *refs: sum_kernel(shards, *refs),
        out_shape=jax.ShapeDtypeStruct(part.shape, part.dtype),
        in_specs=[pl.BlockSpec(memory_space=pltpu.VMEM)],
        out_specs=pl.BlockSpec(memory_space=pltpu.VMEM),
        scratch_shapes=[
            pltpu.VMEM((shards - 1, rows // shards, width), part.dtype),
            pltpu.VMEM(part.shape, part.dtype),
        ]
        + [pltpu.SemaphoreType.DMA((shards - 1,))] * 4,
        compiler_params=pltpu.CompilerParams(
            collective_id=0, has_side_effects=True, vmem_limit_bytes=8 * 2**20
        ),
        cost_estimate=pl.CostEstimate(
            flops=part.size, bytes_accessed=4 * part.size * 4, transcendentals=0
        ),
    )(part)


def gather_kernel(
    shards, meta_ref, held_ref, features_ref, out_ref, all_meta_ref,
    kept_ref, meta_in_ref, own_sem, meta_sent, meta_got, line_sent, line_got, pair_sent, pair_got,
):
    block_rows, block_size, _ = features_ref.shape
    places = shards // 2
    me = lax.axis_index("row")
    at, side = me // 2, lax.rem(me, 2)
    other = 2 * at + 1 - side
    late = max(1, block_rows // 7)
    early = block_rows - late
    cuts = [early * i // 3 for i in range(4)]
    ranges = [pl.ds(a, b - a) for a, b in zip(cuts, cuts[1:])] + [pl.ds(early, late)]
    last = len(ranges) - 1
    streams = [(i, False) for i in range(len(ranges))] + [(last, True)]

    barrier = pltpu.get_barrier_semaphore()
    peers = [lax.rem(me + d, shards) for d in range(1, shards)]
    for peer in peers:
        pl.semaphore_signal(
            barrier, inc=1, device_id={"row": peer}, device_id_type=pl.DeviceIdType.MESH
        )

    def keep(b, carry):
        rows = features_ref[b].astype(jnp.float32)
        hit = held_rows(held_ref, b, block_size)
        kept_ref[b] = jnp.where(hit, 0.0, rows).astype(kept_ref.dtype)
        return carry

    own = pltpu.make_async_copy(kept_ref, out_ref.at[me], own_sem)

    def remote(src, dst, sent, got, peer):
        return pltpu.make_async_remote_copy(
            src_ref=src,
            dst_ref=dst,
            send_sem=sent,
            recv_sem=got,
            device_id={"row": peer},
            device_id_type=pl.DeviceIdType.MESH,
        )

    def piece(origin, part):
        return out_ref.at[origin, ranges[part]]

    def along(way, hop, n, origin_at):
        part, crossed = streams[n]
        origin = 2 * origin_at + (1 - side if crossed else side)
        src = kept_ref.at[ranges[part]] if hop == 1 and not crossed else piece(origin, part)
        k = (0 if way > 0 else 1, hop - 1, n)
        return remote(src, piece(origin, part), line_sent.at[k], line_got.at[k], me + 2 * way)

    def across(way, hop, part, origin_at):
        origin = 2 * origin_at + side
        src = kept_ref.at[ranges[part]] if hop == 0 else piece(origin, part)
        k = (0 if way > 0 else 1, hop, part)
        return remote(src, piece(origin, part), pair_sent.at[k], pair_got.at[k], other)

    def ahead(way, hops=1):
        return (at + way * hops >= 0) & (at + way * hops < places)

    def start_line(way, n):
        @pl.when(ahead(way))
        def _():
            along(way, 1, n, at).start()

    order = [last] + list(range(last))
    for part in order:
        first = early if part == last else cuts[part]
        lax.fori_loop(first, first + ranges[part].size, keep, 0)
        if part == last:
            pl.semaphore_wait(barrier, shards - 1)
        across(1, 0, part, at).start()
        for way in (1, -1):
            start_line(way, part)
    metas = [
        remote(meta_ref, meta_in_ref.at[me], meta_sent.at[d], meta_got.at[d], peer)
        for d, peer in enumerate(peers)
    ]
    for copy in metas:
        copy.start()
    own.start()
    across(1, 0, last, at).wait_recv()
    for way in (1, -1):
        start_line(way, len(streams) - 1)

    walk = [last] + list(range(last)) + [len(streams) - 1]
    for hop in range(1, places):
        for n in walk:
            part, crossed = streams[n]
            for way in (1, -1):

                @pl.when(ahead(-way, hop))
                def _():
                    along(way, hop, n, at - way * hop).wait_recv()
                    if part != last:
                        across(way, hop, part, at - way * hop).start()
                    if hop < places - 1:

                        @pl.when(ahead(way))
                        def _():
                            along(way, hop + 1, n, at - way * hop).start()

    for part in range(last):
        across(1, 0, part, at).wait_recv()
    for part in range(last + 1):
        across(1, 0, part, at).wait_send()
    for way in (1, -1):
        for n in range(len(streams)):

            @pl.when(ahead(way))
            def _():
                along(way, 1, n, at).wait_send()

    for hop in range(1, places):
        for way in (1, -1):

            @pl.when(ahead(-way, hop))
            def _():
                for part in range(last):
                    across(way, hop, part, at - way * hop).wait()
                if hop < places - 1:

                    @pl.when(ahead(way))
                    def _():
                        for n in range(len(streams)):
                            along(way, hop + 1, n, at - way * hop).wait_send()

    for copy in metas:
        copy.wait()
    own.wait()
    all_meta_ref[...] = meta_in_ref[...]
    all_meta_ref[me] = meta_ref[...]


def gather_kept(meta, held_out, features, shards):
    block_rows, block_size, width = features.shape
    streams, places = 5, shards // 2
    return pl.pallas_call(
        lambda *refs: gather_kernel(shards, *refs),
        out_shape=(
            jax.ShapeDtypeStruct((shards, *features.shape), features.dtype),
            jax.ShapeDtypeStruct((shards, *meta.shape), meta.dtype),
        ),
        in_specs=[pl.BlockSpec(memory_space=pltpu.VMEM)] * 3,
        out_specs=(
            pl.BlockSpec(memory_space=pl.ANY),
            pl.BlockSpec(memory_space=pltpu.VMEM),
        ),
        scratch_shapes=[
            pltpu.VMEM(features.shape, features.dtype),
            pltpu.VMEM((shards, *meta.shape), meta.dtype),
            pltpu.SemaphoreType.DMA,
            pltpu.SemaphoreType.DMA((shards - 1,)),
            pltpu.SemaphoreType.DMA((shards - 1,)),
            pltpu.SemaphoreType.DMA((2, places, streams)),
            pltpu.SemaphoreType.DMA((2, places, streams)),
            pltpu.SemaphoreType.DMA((2, places, streams)),
            pltpu.SemaphoreType.DMA((2, places, streams)),
        ],
        compiler_params=pltpu.CompilerParams(
            collective_id=1, has_side_effects=True, vmem_limit_bytes=VMEM_LIMIT
        ),
        cost_estimate=pl.CostEstimate(
            flops=0, bytes_accessed=30 * shards * features.size, transcendentals=0
        ),
    )(meta, held_out, features)


def lane_pad(x):
    return jnp.pad(x, ((0, 0), (0, -x.shape[1] % 128)))


def body(features, blocks, block_ptr, block_col, held_out, weight, cotangent):
    shards = lax.axis_size("row")
    my_feat = lax.axis_index("feat")
    rows_dev, width_dev = features.shape
    slot_count = blocks.shape[0]
    block_size = blocks.shape[2]
    block_rows = block_ptr.shape[1] - 1
    peer_cap = (slot_count + shards - 1) // shards
    buffer_len = shards * peer_cap
    bf16, f32 = jnp.bfloat16, jnp.float32

    slots = jnp.arange(slot_count, dtype=jnp.int32)
    live = slots < block_ptr[0, block_rows]
    columns = block_col[0]
    source = jnp.where(live, columns // block_rows, 0)
    local = jnp.where(live, columns % block_rows, 0)
    block_row = jnp.sum(
        (slots[:, None] >= block_ptr[0, 1:block_rows][None, :]).astype(jnp.int32), axis=1
    )
    earlier = (
        (source[:, None] == source[None, :]) & live[None, :] & (slots[None, :] < slots[:, None])
    )
    rank = jnp.sum(earlier.astype(jnp.int32), axis=1)
    position = jnp.where(live, source * peer_cap + rank, -1)
    places = jnp.arange(buffer_len, dtype=jnp.int32)
    match = (places[:, None] == position[None, :]).astype(jnp.int32)
    wanted = jnp.sum(match * (local[None, :] + 1), axis=1) - 1
    slot_at = jnp.sum(match * slots[None, :], axis=1)
    brow_at = jnp.sum(match * block_row[None, :], axis=1)

    block_shape = (block_size, width_dev)
    feature_blocks = features.reshape(block_rows, *block_shape)
    held = held_out
    dense = jnp.concatenate([cotangent, weight], axis=0)
    dense_piece = lax.all_gather(dense, "feat", axis=1, tiled=True)
    full_blocks = lax.all_gather(blocks, "feat", axis=1, tiled=True)
    whole = shards > 2 and shards % 2 == 0 and block_rows <= 2 * peer_cap
    if whole:
        span = max(block_rows + 1, slot_count)
        tables = jnp.concatenate(
            [
                jnp.pad(block_ptr, ((0, 0), (0, span - block_rows - 1))),
                jnp.pad(block_col, ((0, 0), (0, span - slot_count))),
            ],
            axis=0,
        )
        meta = lane_pad(jnp.pad(tables, ((0, 6), (0, 0))))
        gathered, all_meta = gather_kept(meta, held, feature_blocks, shards)
        all_meta, dense_piece, full_blocks = lax.optimization_barrier(
            (all_meta, dense_piece, full_blocks)
        )
        me = lax.axis_index("row")
        all_col = all_meta[:, 1, :slot_count]
        all_live = slots[None, :] < all_meta[:, 0, block_rows][:, None]
        named = all_live & (all_col // block_rows == me)
        ahead = (slots[:, None] < slots[None, :]).astype(f32)
        order = jnp.dot(named.astype(f32), ahead, preferred_element_type=f32).astype(jnp.int32)
        at_rank = named[:, None, :] & (
            order[:, None, :] == jnp.arange(peer_cap, dtype=jnp.int32)[None, :, None]
        )
        asked = jnp.sum(
            jnp.where(at_rank, all_col[:, None, :] % block_rows + 1, 0), axis=2
        ).reshape(buffer_len) - 1
        arrived = gathered.reshape(shards * block_rows, *block_shape)
        found = jnp.where(live, columns, 0)
    else:
        asked = lax.all_to_all(wanted, "row", split_axis=0, concat_axis=0, tiled=True)
        outgoing = local_call(
            pack_kernel,
            (asked,),
            (held, feature_blocks),
            jax.ShapeDtypeStruct((buffer_len, *block_shape), bf16),
            (pltpu.VMEM((block_rows, *block_shape), bf16),),
        )
        arrived = lax.all_to_all(outgoing, "row", split_axis=0, concat_axis=0, tiled=True)
        found = jnp.maximum(position, 0)
    cot_piece, weight_piece = dense_piece[:rows_dev], dense_piece[rows_dev:]
    weight_mine = lax.dynamic_slice_in_dim(weight_piece, my_feat * width_dev, width_dev, 0)
    agg_grad = lax.dot_general(
        cot_piece, weight_mine, (((1,), (1,)), ((), ())), preferred_element_type=f32
    ).astype(bf16)
    sending = local_call(
        contribution_kernel,
        (slot_at, brow_at),
        (full_blocks, agg_grad.reshape(block_rows, *block_shape)),
        jax.ShapeDtypeStruct((buffer_len, *block_shape), bf16),
        flops=2 * buffer_len * block_size * block_size * width_dev,
    )
    returned = lax.all_to_all(sending, "row", split_axis=0, concat_axis=0, tiled=True)

    aggregated = local_call(
        forward_kernel,
        (found, jnp.where(live, block_row, block_rows)),
        (full_blocks, arrived),
        jax.ShapeDtypeStruct((block_rows, *block_shape), bf16),
        (pltpu.VMEM((block_rows + 1, *block_shape), f32),),
        flops=2 * slot_count * block_size * block_size * width_dev,
    ).reshape(rows_dev, width_dev)
    piece = lax.all_gather(aggregated, "feat", axis=1, tiled=True)
    layer_out = jnp.dot(piece, weight, preferred_element_type=f32).astype(bf16)
    grad_part = lax.dot_general(
        piece, cotangent, (((0,), (0,)), ((), ())), preferred_element_type=f32
    )
    grad_part, layer_out = lax.optimization_barrier((grad_part, layer_out))
    grad_total = row_sum(grad_part)
    returned, grad_total = lax.optimization_barrier((returned, grad_total))
    weight_grad = grad_total * (1.0 / jnp.sqrt(f32(rows_dev * shards)))
    feature_grad = local_call(
        collect_kernel,
        (asked,),
        (held, returned),
        jax.ShapeDtypeStruct((block_rows, *block_shape), bf16),
        (pltpu.VMEM((block_rows + 1, *block_shape), f32),),
    ).reshape(rows_dev, width_dev)
    return (layer_out, feature_grad, weight_grad)


def solution(mesh):
    in_specs = (
        P("row", "feat"),
        P("row", "feat", None),
        P("row", None),
        P("row", None),
        P("row", None),
        P(None, "feat"),
        P("row", "feat"),
    )
    out_specs = (P("row", "feat"), P("row", "feat"), P(None, "feat"))
    return jax.shard_map(body, mesh=mesh, in_specs=in_specs, out_specs=out_specs, check_vma=False)
```
